32 devices in a mesh: groups: 2 (over y), wide: 4 (over z), narrow: 4 (over x, core).
Axes of the slice: x: 2, y: 2, z: 4, core: 2. Of those that a mesh axis runs over, the one named last changes fastest.
Arguments:
- tiles: bfloat16 [8, 4, 224, 128, 128], P(('groups', 'wide'), 'narrow'), parts along dimension 0, may hold values from 0.19921875 to 20
- tile_rows: int32 [8, 4, 224], P(('groups', 'wide'), 'narrow'), parts along dimension 0, may hold values from 0 to 15, as said below
- tile_cols: int32 [8, 4, 224], P(('groups', 'wide'), 'narrow'), parts along dimension 0, may hold values from 0 to 31
- tile_live: int32 [8, 4, 224], P(('groups', 'wide'), 'narrow'), parts along dimension 0, may hold values 0 or 1
- omega: bfloat16 [32768, 256], P(('groups', 'narrow')), parts along dimension 0, may hold values from -0.0625 to 0.0625
- psi: bfloat16 [512, 16384], P(None, ('groups', 'wide')), parts along dimension 1, may hold values from -0.09375 to 0.09375
Outputs:
- range_sketch: float32 [16384, 256], P(('groups', 'wide', 'narrow')), parts along dimension 0
- corange_sketch: float32 [512, 32768], P('wide', ('groups', 'narrow')), parts along dimension 1
The draws below stay inside these ranges and needn't reach their ends.
There are 2 independent parts, one for each index of `groups`. The reference program is written for one: setup_inputs(seed, part) draws one part's arguments, and reference() takes and returns one part's arrays. A program takes and returns all parts, laid end to end along the dimension named above; each array names one. Nothing has to cross between parts.
Inputs may be any that keep to these rules, and one draw needn't show every extreme that they name: Within one device's slots no two slots share the same pair (tile_rows, tile_cols).
All inputs are finite; a program needn't handle non-finite values. No bound on the sum of `tile_live` on one device may be relied on, other than what follows from the above.
Results may differ from the reference program's by a relative error of at most 0.005.
Values sent between devices are 32-bit elements; how exact they have to be, the bound alone decides.
A program may use at most 128 MiB of HBM per device.

```python
import math
import jax
import jax.numpy as jnp
from jax import lax

TILE = 128
TILE_ROWS_DEV = 16
TILE_COLS_DEV = 32
RANK = 256
CORANK = 512
SLOTS = 224
NR = 8192
NC = 16384
N_WIDE = 4
N_NARROW = 4


def slot_positions(key):
    keys = jax.random.split(key, N_WIDE * N_NARROW)
    perms = jax.vmap(lambda k: jax.random.permutation(k, TILE_ROWS_DEV * TILE_COLS_DEV))(keys)
    return perms[:, :SLOTS].reshape(N_WIDE, N_NARROW, SLOTS).astype(jnp.int32)


def draw_tile_rows(key, part):
    return slot_positions(key) // TILE_COLS_DEV


def draw_tile_cols(key, part):
    return slot_positions(key) % TILE_COLS_DEV


def plant(drawn, rng, least, top_value):
    index_at = [jax.random.randint(jax.random.fold_in(rng, axis), (), 0, length) for axis, length in enumerate(drawn.shape)]
    widest = drawn.shape.index(max(drawn.shape))
    neighbour = index_at[:widest] + [(index_at[widest] + 1) % drawn.shape[widest]] + index_at[widest + 1:]
    return drawn.at[tuple(index_at)].set(least).at[tuple(neighbour)].set(top_value)


def strengthened(array, key, source, target, parts, factor):
    owner, partner = [(jnp.arange(array.shape[position]) // (array.shape[position] // parts)).reshape([-1 if axis == position else 1 for axis in range(array.ndim)]) for position in (source, target)]
    chosen = jax.random.permutation(key, parts)[partner]
    strong = (owner == chosen) | (owner == (partner + parts // 2) % parts)
    return jnp.where(strong, factor * array, array)


def levels(key, shape, pieces, least, top_value):
    def one(axis_at, shards_of):
        draws = jax.random.uniform(jax.random.fold_in(jax.random.fold_in(key, 6), axis_at), (shards_of,), jnp.float32, least / len(pieces), top_value / len(pieces))
        return jnp.repeat(jnp.exp(draws), shape[axis_at] // shards_of).reshape((-1,) + (1,) * (len(shape) - axis_at - 1))

    gain = one(*pieces[0])
    for cut in pieces[1:]:
        gain = gain * one(*cut)
    return gain


def gaussian_with(own_key, extent, spread, most, shards, heavy, kind=jnp.bfloat16):
    array = spread * jax.random.normal(own_key, extent, jnp.float32)
    if shards:
        array = array * levels(own_key, extent, shards, -0.22, 0.18)
    return jnp.clip(strengthened(array, jax.random.fold_in(own_key, 3), *heavy), -most, most).astype(kind)


def setup_inputs(seed: int = 0, part: int = 0) -> dict:
    key_list = jax.random.split(jax.random.key(seed), 7)
    part_keys = jax.random.split(jax.random.fold_in(key_list[6], part), 7)
    tiles = jnp.clip(jnp.exp(math.log(20.0) - 4.609084 * jax.random.uniform(part_keys[0], (N_WIDE, N_NARROW, SLOTS, TILE, TILE), jnp.float32) ** levels(part_keys[0], (N_WIDE, N_NARROW, SLOTS, TILE, TILE), ((0, 4), (1, 4)), -0.2, 0.2)), 0.19921875, 20.0).astype(jnp.bfloat16)
    tile_rows = draw_tile_rows(jax.random.fold_in(jax.random.fold_in(key_list[6], part), 71), part)
    tile_cols = draw_tile_cols(jax.random.fold_in(jax.random.fold_in(key_list[6], part), 71), part)
    tile_live = plant((jax.random.randint(part_keys[3], (N_WIDE, N_NARROW, SLOTS), 0, 4) < 3).astype(jnp.int32), jax.random.fold_in(part_keys[3], 1), 0, 1)
    omega = gaussian_with(part_keys[4], (NC, RANK), NC ** -0.5, 0.0625, ((0, 4),), (0, 1, 4, 2.0))
    psi = gaussian_with(part_keys[5], (CORANK, NR), NR ** -0.5, 0.09375, ((1, 4),), (1, 0, 4, 2.0))
    return {"tiles": tiles, "tile_rows": tile_rows, "tile_cols": tile_cols, "tile_live": tile_live, "omega": omega, "psi": psi}


def reference(tiles, tile_rows, tile_cols, tile_live, omega, psi):
    wide_count, narrow_count, slots, tile, _ = tiles.shape
    grow = (jnp.arange(wide_count, dtype=jnp.int32)[:, None, None] * TILE_ROWS_DEV + tile_rows).astype(jnp.int32)
    gcol = (jnp.arange(narrow_count, dtype=jnp.int32)[None, :, None] * TILE_COLS_DEV + tile_cols).astype(jnp.int32)
    grow = grow.reshape(wide_count * narrow_count, slots)
    gcol = gcol.reshape(wide_count * narrow_count, slots)
    livef = tile_live.reshape(wide_count * narrow_count, slots).astype(jnp.float32)
    values = jnp.log(jnp.maximum(tiles.astype(jnp.float32), 1.0)).astype(jnp.bfloat16)
    values = values.reshape(wide_count * narrow_count, slots, tile, tile)
    omega_blocks = omega.astype(jnp.float32).reshape(NC // tile, tile, RANK)
    psi_blocks = psi.astype(jnp.float32).reshape(CORANK, NR // tile, tile).transpose(1, 0, 2)

    def visit(carry, block):
        ranges, coranges = carry
        vals, rws, cls, lv = block
        vals = vals.astype(jnp.float32)
        prod = jnp.einsum("sij,sjk->sik", vals, omega_blocks[cls]) * lv[:, None, None]
        ranges = ranges.at[rws].add(prod)
        prodc = jnp.einsum("sli,sij->slj", psi_blocks[rws], vals) * lv[:, None, None]
        coranges = coranges.at[cls].add(prodc)
        return (ranges, coranges), None

    init = (jnp.zeros((NR // tile, tile, RANK), jnp.float32), jnp.zeros((NC // tile, CORANK, tile), jnp.float32))
    (ranges, coranges), _ = lax.scan(visit, init, (values, grow, gcol, livef))
    return ranges.reshape(NR, RANK), coranges.transpose(1, 0, 2).reshape(CORANK, NC)
```

```python
import functools

import jax
import jax.numpy as jnp
from jax import lax
from jax.experimental import pallas as pl
from jax.experimental.pallas import tpu as pltpu
from jax.sharding import PartitionSpec as P

MESH = pl.DeviceIdType.MESH
F32 = jnp.float32
BF16 = jnp.bfloat16


def kernel(
    nw, nn, width, depth,
    slot_at, tiles_hbm, psi_hbm, omega_hbm, range_hbm, corange_hbm,
    tiles, psi, omega, dense, part, arrived, rpart, rarrived,
    in_sem, send_sem, recv_sem, rsend_sem, rrecv_sem, out_sem, rout_sem,
):
    me = lax.axis_index("wide")
    mine = lax.axis_index("narrow")
    slots, tile = tiles_hbm.shape[0], tiles_hbm.shape[1]
    corank, rows = psi.shape
    chunks = part.shape[0]
    share = corank // nw
    rblock = rows // nn
    row_blocks = rows // tile
    per_chunk = width // tile

    in_copies = [
        pltpu.make_async_copy(tiles_hbm, tiles.at[pl.ds(0, slots)], in_sem.at[0]),
        pltpu.make_async_copy(psi_hbm, psi, in_sem.at[1]),
        pltpu.make_async_copy(omega_hbm, omega, in_sem.at[2]),
    ]
    for copy in in_copies:
        copy.start()

    barrier = pltpu.get_barrier_semaphore()

    @pl.when(me > 0)
    def _():
        pl.semaphore_signal(barrier, inc=1, device_id={"wide": me - 1}, device_id_type=MESH)

    @pl.when(me < nw - 1)
    def _():
        pl.semaphore_signal(barrier, inc=1, device_id={"wide": me + 1}, device_id_type=MESH)

    for d in range(1, nn):
        pl.semaphore_signal(
            barrier, inc=1, device_id={"narrow": lax.rem(mine + d, nn)}, device_id_type=MESH
        )
    tiles[slots] = jnp.ones((tile, tile), BF16)
    rpart[...] = jnp.zeros_like(rpart)
    near = jnp.where(me > 0, 1, 0) + jnp.where(me < nw - 1, 1, 0)
    pl.semaphore_wait(barrier, nn - 1 + near)

    def own(j, c):
        return part.at[c, pl.ds(pl.multiple_of(j * share, share), share)]

    def rightward(j, c):
        return pltpu.make_async_remote_copy(
            src_ref=own(j, c), dst_ref=arrived.at[j, c],
            send_sem=send_sem.at[j, c], recv_sem=recv_sem.at[j, c],
            device_id={"wide": me + 1}, device_id_type=MESH,
        )

    def leftward(j, c):
        slot = jnp.where(j == me - 1, nw, j)
        return pltpu.make_async_remote_copy(
            src_ref=own(j, c), dst_ref=arrived.at[slot, c],
            send_sem=send_sem.at[j, c], recv_sem=recv_sem.at[slot, c],
            device_id={"wide": me - 1}, device_id_type=MESH,
        )

    def await_arrival(slot, c):
        pltpu.make_async_copy(arrived.at[slot, c], arrived.at[slot, c], recv_sem.at[slot, c]).wait()

    def add_arrived(j, slot, c):
        at = pl.ds(pl.multiple_of(j * share, share), share)
        part[c, at, :] = part[c, at, :] + arrived[slot, c]

    in_copies[0].wait()
    in_copies[1].wait()
    in_copies[2].wait()

    def chunk_step(c, carry):
        def place(r, carry):
            for q in range(per_chunk):
                value = tiles[slot_at[(c * per_chunk + q) * row_blocks + r]]
                value = jnp.log(jnp.maximum(value.astype(F32), 1.0)).astype(BF16)
                dense[pl.ds(pl.multiple_of(r * tile, tile), tile), q * tile : (q + 1) * tile] = value
            return carry

        lax.fori_loop(0, row_blocks, place, 0)

        def corange_rows(m, carry):
            at = pl.ds(pl.multiple_of(m * depth, depth), depth)
            part[c, at, :] = jnp.dot(psi[at, :], dense[...], preferred_element_type=F32)
            return carry

        lax.fori_loop(0, corank // depth, corange_rows, 0)

        @pl.when(me == 0)
        def _():
            rightward(nw - 1, c).start()

        @pl.when(me == nw - 1)
        def _():
            leftward(0, c).start()

        chosen = omega[pl.ds(pl.multiple_of(c * width, width), width), :]

        def range_rows(m, carry):
            at = pl.ds(pl.multiple_of(m * depth, depth), depth)
            rpart[at, :] = rpart[at, :] + jnp.dot(dense[at, :], chosen, preferred_element_type=F32)
            return carry

        lax.fori_loop(0, rows // depth, range_rows, 0)
        return carry

    lax.fori_loop(0, chunks, chunk_step, 0)

    def range_copy(d):
        to = lax.rem(mine + d, nn)
        return pltpu.make_async_remote_copy(
            src_ref=rpart.at[pl.ds(pl.multiple_of(to * rblock, rblock), rblock)],
            dst_ref=rarrived.at[d - 1],
            send_sem=rsend_sem.at[d - 1], recv_sem=rrecv_sem.at[d - 1],
            device_id={"narrow": to}, device_id_type=MESH,
        )

    for d in range(1, nn):
        range_copy(d).start()

    def line_step(k, carry):
        s, c = k // chunks, k % chunks
        right_share = nw - 1 - s
        left_share = s

        @pl.when(jnp.logical_and(me < right_share, jnp.logical_or(me > 0, s > 0)))
        def _():
            @pl.when(me > 0)
            def _():
                await_arrival(right_share, c)
                add_arrived(right_share, right_share, c)

            rightward(right_share, c).start()

        @pl.when(jnp.logical_and(me > left_share, jnp.logical_or(me < nw - 1, s > 0)))
        def _():
            @pl.when(me < nw - 1)
            def _():
                await_arrival(left_share, c)
                add_arrived(left_share, left_share, c)

            leftward(left_share, c).start()

        return carry

    lax.fori_loop(0, (nw - 1) * chunks, line_step, 0)

    at = pl.ds(pl.multiple_of(mine * rblock, rblock), rblock)
    for d in range(1, nn):
        range_copy(d).wait_recv()
    total = rpart[at, :]
    for d in range(1, nn):
        total = total + rarrived[d - 1]
    rpart[at, :] = total
    range_out = pltpu.make_async_copy(rpart.at[at], range_hbm, rout_sem)
    range_out.start()

    def share_out(c):
        return pltpu.make_async_copy(
            own(me, c), corange_hbm.at[:, pl.ds(pl.multiple_of(c * width, width), width)], out_sem.at[c]
        )

    def finish(c, carry):
        @pl.when(me < nw - 1)
        def _():
            await_arrival(nw, c)
            add_arrived(me, nw, c)

        @pl.when(me > 0)
        def _():
            await_arrival(me, c)
            add_arrived(me, me, c)

        share_out(c).start()
        return carry

    lax.fori_loop(0, chunks, finish, 0)

    def drain(k, carry):
        j, c = k // chunks, k % chunks

        @pl.when(j != me)
        def _():
            pltpu.make_async_copy(own(j, c), own(j, c), send_sem.at[j, c]).wait()

        return carry

    lax.fori_loop(0, nw * chunks, drain, 0)

    def drain_out(c, carry):
        share_out(c).wait()
        return carry

    lax.fori_loop(0, chunks, drain_out, 0)
    for d in range(1, nn):
        range_copy(d).wait_send()
    range_out.wait()


def on_device(nw, nn, tiles, tile_rows, tile_cols, tile_live, omega, psi):
    slots, tile = tiles.shape[2], tiles.shape[3]
    rank, corank = omega.shape[1], psi.shape[0]
    rows, cols = psi.shape[1], omega.shape[0]
    row_blocks, col_blocks = rows // tile, cols // tile
    width = 2 * tile
    depth = 2 * tile
    chunks = cols // width
    share, rblock = corank // nw, rows // nn

    place = jnp.where(tile_live > 0, tile_cols * row_blocks + tile_rows, -1).reshape(slots)
    hit = place[None, :] == jnp.arange(row_blocks * col_blocks, dtype=jnp.int32)[:, None]
    back = jnp.arange(slots, dtype=jnp.int32) - slots
    slot_at = slots + jnp.sum(jnp.where(hit, back[None, :], 0), axis=1, dtype=jnp.int32)

    return pl.pallas_call(
        functools.partial(kernel, nw, nn, width, depth),
        out_shape=(
            jax.ShapeDtypeStruct((rblock, rank), F32),
            jax.ShapeDtypeStruct((share, cols), F32),
        ),
        in_specs=[pl.BlockSpec(memory_space=pltpu.SMEM)] + [pl.BlockSpec(memory_space=pl.ANY)] * 3,
        out_specs=(pl.BlockSpec(memory_space=pl.ANY),) * 2,
        scratch_shapes=[
            pltpu.VMEM((slots + 1, tile, tile), BF16),
            pltpu.VMEM((corank, rows), BF16),
            pltpu.VMEM((cols, rank), BF16),
            pltpu.VMEM((rows, width), BF16),
            pltpu.VMEM((chunks, corank, width), F32),
            pltpu.VMEM((nw + 1, chunks, share, width), F32),
            pltpu.VMEM((rows, rank), F32),
            pltpu.VMEM((nn - 1, rblock, rank), F32),
            pltpu.SemaphoreType.DMA((3,)),
            pltpu.SemaphoreType.DMA((nw, chunks)),
            pltpu.SemaphoreType.DMA((nw + 1, chunks)),
            pltpu.SemaphoreType.DMA((nn - 1,)),
            pltpu.SemaphoreType.DMA((nn - 1,)),
            pltpu.SemaphoreType.DMA((chunks,)),
            pltpu.SemaphoreType.DMA,
        ],
        compiler_params=pltpu.CompilerParams(
            collective_id=0, has_side_effects=True, vmem_limit_bytes=52 << 20
        ),
        name="sketch",
    )(slot_at, tiles.reshape(slots, tile, tile), psi, omega)


def solution(mesh):
    in_specs = (
        P(("groups", "wide"), "narrow", None, None, None),
        P(("groups", "wide"), "narrow", None),
        P(("groups", "wide"), "narrow", None),
        P(("groups", "wide"), "narrow", None),
        P(("groups", "narrow"), None),
        P(None, ("groups", "wide")),
    )
    out_specs = (P(("groups", "wide", "narrow"), None), P("wide", ("groups", "narrow")))
    return jax.shard_map(
        functools.partial(on_device, mesh.shape["wide"], mesh.shape["narrow"]),
        mesh=mesh, in_specs=in_specs, out_specs=out_specs, check_vma=False,
    )
```

```python
import functools

import jax
import jax.numpy as jnp
from jax import lax
from jax.experimental import pallas as pl
from jax.experimental.pallas import tpu as pltpu
from jax.sharding import PartitionSpec as P

MESH = pl.DeviceIdType.MESH
F32 = jnp.float32
BF16 = jnp.bfloat16


def kernel(
    nw, nn, width, depth, tall, window, lag, late,
    slot_at, tiles_hbm, psi_hbm, omega_hbm, range_hbm, corange_hbm,
    tiles, psi, omega, dense, part, arrived, rpart, rarrived,
    in_sem, send_sem, recv_sem, rsend_sem, rrecv_sem, out_sem, rout_sem,
):
    me = lax.axis_index("wide")
    mine = lax.axis_index("narrow")
    slots, tile = tiles_hbm.shape[0], tiles_hbm.shape[1]
    corank, rows = psi.shape
    chunks = part.shape[0]
    share = corank // nw
    rblock = rows // nn
    row_blocks = rows // tile
    per_chunk = width // tile

    in_copies = [
        pltpu.make_async_copy(tiles_hbm, tiles.at[pl.ds(0, slots)], in_sem.at[0]),
        pltpu.make_async_copy(psi_hbm, psi, in_sem.at[1]),
        pltpu.make_async_copy(omega_hbm, omega, in_sem.at[2]),
    ]
    for copy in in_copies:
        copy.start()

    barrier = pltpu.get_barrier_semaphore()

    @pl.when(me > 0)
    def _():
        pl.semaphore_signal(barrier, inc=1, device_id={"wide": me - 1}, device_id_type=MESH)

    @pl.when(me < nw - 1)
    def _():
        pl.semaphore_signal(barrier, inc=1, device_id={"wide": me + 1}, device_id_type=MESH)

    for d in range(1, nn):
        pl.semaphore_signal(
            barrier, inc=1, device_id={"narrow": lax.rem(mine + d, nn)}, device_id_type=MESH
        )
    tiles[slots] = jnp.ones((tile, tile), BF16)
    rpart[...] = jnp.zeros_like(rpart)
    near = jnp.where(me > 0, 1, 0) + jnp.where(me < nw - 1, 1, 0)
    pl.semaphore_wait(barrier, nn - 1 + near)

    def own(j, c):
        return part.at[c, pl.ds(pl.multiple_of(j * share, share), share)]

    def rightward(j, c):
        return pltpu.make_async_remote_copy(
            src_ref=own(j, c), dst_ref=arrived.at[j, c],
            send_sem=send_sem.at[j, c], recv_sem=recv_sem.at[j, c],
            device_id={"wide": me + 1}, device_id_type=MESH,
        )

    def leftward(j, c):
        slot = jnp.where(j == me - 1, nw, j)
        return pltpu.make_async_remote_copy(
            src_ref=own(j, c), dst_ref=arrived.at[slot, c],
            send_sem=send_sem.at[j, c], recv_sem=recv_sem.at[slot, c],
            device_id={"wide": me - 1}, device_id_type=MESH,
        )

    def await_arrival(slot, c):
        pltpu.make_async_copy(arrived.at[slot, c], arrived.at[slot, c], recv_sem.at[slot, c]).wait()

    def add_arrived(j, slot, c):
        at = pl.ds(pl.multiple_of(j * share, share), share)
        part[c, at, :] = part[c, at, :] + arrived[slot, c]

    def await_sent(k, left):
        s, c = k // chunks, k % chunks
        j = s if left else nw - 1 - s
        pltpu.make_async_copy(own(j, c), own(j, c), send_sem.at[j, c]).wait()

    def make_room(k, left=False):
        @pl.when(k >= chunks)
        def _():
            await_sent(k - window, left)

    pieces = (nw - 1) * chunks

    def line_step(k, carry):
        nearer = 2 * me < nw
        k_right = jnp.where(nearer, k, k - late)
        k_left = jnp.where(nearer, k - late, k)

        def forward(k, left):
            within = jnp.logical_and(k >= 0, k < pieces)
            s, c = jnp.maximum(k, 0) // chunks, jnp.maximum(k, 0) % chunks
            share_at = s if left else nw - 1 - s
            passes = me > share_at if left else me < share_at
            inner = me < nw - 1 if left else me > 0

            @pl.when(within & passes & (inner | (s > 0)))
            def _():
                @pl.when(inner)
                def _():
                    await_arrival(share_at, c)
                    add_arrived(share_at, share_at, c)

                make_room(k, left)
                (leftward if left else rightward)(share_at, c).start()

        forward(k_right, False)
        forward(k_left, True)
        return carry

    in_copies[0].wait()
    in_copies[1].wait()
    in_copies[2].wait()

    def chunk_step(c, carry):
        def place(r, carry):
            for q in range(per_chunk):
                value = tiles[slot_at[(c * per_chunk + q) * row_blocks + r]]
                value = jnp.log(jnp.maximum(value.astype(F32), 1.0)).astype(BF16)
                dense[pl.ds(pl.multiple_of(r * tile, tile), tile), q * tile : (q + 1) * tile] = value
            return carry

        lax.fori_loop(0, row_blocks, place, 0)

        def corange_rows(m, carry):
            at = pl.ds(pl.multiple_of(m * depth, depth), depth)
            part[c, at, :] = jnp.dot(psi[at, :], dense[...], preferred_element_type=F32)
            return carry

        lax.fori_loop(0, corank // depth, corange_rows, 0)

        @pl.when(me == 0)
        def _():
            rightward(nw - 1, c).start()

        @pl.when(me == nw - 1)
        def _():
            leftward(0, c).start()

        @pl.when(c >= lag)
        def _():
            line_step(c - lag, 0)

        chosen = omega[pl.ds(pl.multiple_of(c * width, width), width), :]

        def range_rows(m, carry):
            at = pl.ds(pl.multiple_of(m * tall, tall), tall)
            rpart[at, :] = rpart[at, :] + jnp.dot(dense[at, :], chosen, preferred_element_type=F32)
            return carry

        lax.fori_loop(0, rows // tall, range_rows, 0)
        return carry

    lax.fori_loop(0, chunks, chunk_step, 0)

    def range_copy(d):
        to = lax.rem(mine + d, nn)
        return pltpu.make_async_remote_copy(
            src_ref=rpart.at[pl.ds(pl.multiple_of(to * rblock, rblock), rblock)],
            dst_ref=rarrived.at[d - 1],
            send_sem=rsend_sem.at[d - 1], recv_sem=rrecv_sem.at[d - 1],
            device_id={"narrow": to}, device_id_type=MESH,
        )

    for d in range(1, nn):
        range_copy(d).start()

    lax.fori_loop(chunks - lag, pieces + late, line_step, 0)

    at = pl.ds(pl.multiple_of(mine * rblock, rblock), rblock)
    for d in range(1, nn):
        range_copy(d).wait_recv()
    total = rpart[at, :]
    for d in range(1, nn):
        total = total + rarrived[d - 1]
    rpart[at, :] = total
    range_out = pltpu.make_async_copy(rpart.at[at], range_hbm, rout_sem)
    range_out.start()

    def share_out(c):
        return pltpu.make_async_copy(
            own(me, c), corange_hbm.at[:, pl.ds(pl.multiple_of(c * width, width), width)], out_sem.at[c]
        )

    def finish(c, carry):
        @pl.when(me < nw - 1)
        def _():
            await_arrival(nw, c)
            add_arrived(me, nw, c)

        @pl.when(me > 0)
        def _():
            await_arrival(me, c)
            add_arrived(me, me, c)

        share_out(c).start()
        return carry

    lax.fori_loop(0, chunks, finish, 0)

    def drain(k, carry):
        for left, sent in ((False, (nw - 1 - me) * chunks), (True, me * chunks)):
            last = jnp.logical_and(k >= sent - window, k < sent)
            first = jnp.logical_and(k < chunks - window, k < sent)

            @pl.when(jnp.logical_or(first, last))
            def _():
                await_sent(k, left)

        return carry

    lax.fori_loop(0, (nw - 1) * chunks, drain, 0)

    def drain_out(c, carry):
        share_out(c).wait()
        return carry

    lax.fori_loop(0, chunks, drain_out, 0)
    for d in range(1, nn):
        range_copy(d).wait_send()
    range_out.wait()


def on_device(nw, nn, tiles, tile_rows, tile_cols, tile_live, omega, psi):
    slots, tile = tiles.shape[2], tiles.shape[3]
    rank, corank = omega.shape[1], psi.shape[0]
    rows, cols = psi.shape[1], omega.shape[0]
    row_blocks, col_blocks = rows // tile, cols // tile
    width = 4 * tile
    depth = 2 * tile
    tall = rows // 2
    window = 4
    lag = 1
    late = 2
    chunks = cols // width
    share, rblock = corank // nw, rows // nn

    place = jnp.where(tile_live > 0, tile_cols * row_blocks + tile_rows, -1).reshape(slots)
    hit = place[None, :] == jnp.arange(row_blocks * col_blocks, dtype=jnp.int32)[:, None]
    back = jnp.arange(slots, dtype=jnp.int32) - slots
    slot_at = slots + jnp.sum(jnp.where(hit, back[None, :], 0), axis=1, dtype=jnp.int32)

    return pl.pallas_call(
        functools.partial(kernel, nw, nn, width, depth, tall, window, lag, late),
        out_shape=(
            jax.ShapeDtypeStruct((rblock, rank), F32),
            jax.ShapeDtypeStruct((share, cols), F32),
        ),
        in_specs=[pl.BlockSpec(memory_space=pltpu.SMEM)] + [pl.BlockSpec(memory_space=pl.ANY)] * 3,
        out_specs=(pl.BlockSpec(memory_space=pl.ANY),) * 2,
        scratch_shapes=[
            pltpu.VMEM((slots + 1, tile, tile), BF16),
            pltpu.VMEM((corank, rows), BF16),
            pltpu.VMEM((cols, rank), BF16),
            pltpu.VMEM((rows, width), BF16),
            pltpu.VMEM((chunks, corank, width), F32),
            pltpu.VMEM((nw + 1, chunks, share, width), F32),
            pltpu.VMEM((rows, rank), F32),
            pltpu.VMEM((nn - 1, rblock, rank), F32),
            pltpu.SemaphoreType.DMA((3,)),
            pltpu.SemaphoreType.DMA((nw, chunks)),
            pltpu.SemaphoreType.DMA((nw + 1, chunks)),
            pltpu.SemaphoreType.DMA((nn - 1,)),
            pltpu.SemaphoreType.DMA((nn - 1,)),
            pltpu.SemaphoreType.DMA((chunks,)),
            pltpu.SemaphoreType.DMA,
        ],
        compiler_params=pltpu.CompilerParams(
            collective_id=0, has_side_effects=True, vmem_limit_bytes=52 << 20
        ),
        name="sketch",
    )(slot_at, tiles.reshape(slots, tile, tile), psi, omega)


def solution(mesh):
    in_specs = (
        P(("groups", "wide"), "narrow", None, None, None),
        P(("groups", "wide"), "narrow", None),
        P(("groups", "wide"), "narrow", None),
        P(("groups", "wide"), "narrow", None),
        P(("groups", "narrow"), None),
        P(None, ("groups", "wide")),
    )
    out_specs = (P(("groups", "wide", "narrow"), None), P("wide", ("groups", "narrow")))
    return jax.shard_map(
        functools.partial(on_device, mesh.shape["wide"], mesh.shape["narrow"]),
        mesh=mesh, in_specs=in_specs, out_specs=out_specs, check_vma=False,
    )
```

```python
import functools

import jax
import jax.numpy as jnp
from jax import lax
from jax.experimental import pallas as pl
from jax.experimental.pallas import tpu as pltpu
from jax.sharding import PartitionSpec as P

MESH = pl.DeviceIdType.MESH
F32 = jnp.float32
BF16 = jnp.bfloat16


def kernel(
    nw, nn, width, depth, tall, window, lag, late,
    slot_at, tiles_hbm, psi_hbm, omega_hbm, range_hbm, corange_hbm,
    tiles, psi, omega, dense, part, arrived, rpart, rarrived,
    in_sem, send_sem, recv_sem, rsend_sem, rrecv_sem, out_sem, rout_sem,
):
    me = lax.axis_index("wide")
    mine = lax.axis_index("narrow")
    slots, tile = tiles_hbm.shape[0], tiles_hbm.shape[1]
    corank, rows = psi.shape
    chunks = part.shape[0]
    share = corank // nw
    rblock = rows // nn
    row_blocks = rows // tile
    per_chunk = width // tile

    in_copies = [
        pltpu.make_async_copy(tiles_hbm, tiles.at[pl.ds(0, slots)], in_sem.at[0]),
        pltpu.make_async_copy(psi_hbm, psi, in_sem.at[1]),
        pltpu.make_async_copy(omega_hbm, omega, in_sem.at[2]),
    ]
    for copy in in_copies:
        copy.start()

    barrier = pltpu.get_barrier_semaphore()

    @pl.when(me > 0)
    def _():
        pl.semaphore_signal(barrier, inc=1, device_id={"wide": me - 1}, device_id_type=MESH)

    @pl.when(me < nw - 1)
    def _():
        pl.semaphore_signal(barrier, inc=1, device_id={"wide": me + 1}, device_id_type=MESH)

    for d in range(1, nn):
        pl.semaphore_signal(
            barrier, inc=1, device_id={"narrow": lax.rem(mine + d, nn)}, device_id_type=MESH
        )
    tiles[slots] = jnp.ones((tile, tile), BF16)
    rpart[...] = jnp.zeros_like(rpart)
    near = jnp.where(me > 0, 1, 0) + jnp.where(me < nw - 1, 1, 0)
    pl.semaphore_wait(barrier, nn - 1 + near)

    def own(j, c):
        return part.at[c, pl.ds(pl.multiple_of(j * share, share), share)]

    def rightward(j, c):
        return pltpu.make_async_remote_copy(
            src_ref=own(j, c), dst_ref=arrived.at[j, c],
            send_sem=send_sem.at[j, c], recv_sem=recv_sem.at[j, c],
            device_id={"wide": me + 1}, device_id_type=MESH,
        )

    def leftward(j, c):
        slot = jnp.where(j == me - 1, nw, j)
        return pltpu.make_async_remote_copy(
            src_ref=own(j, c), dst_ref=arrived.at[slot, c],
            send_sem=send_sem.at[j, c], recv_sem=recv_sem.at[slot, c],
            device_id={"wide": me - 1}, device_id_type=MESH,
        )

    def await_arrival(slot, c):
        pltpu.make_async_copy(arrived.at[slot, c], arrived.at[slot, c], recv_sem.at[slot, c]).wait()

    def add_arrived(j, slot, c):
        at = pl.ds(pl.multiple_of(j * share, share), share)
        part[c, at, :] = part[c, at, :] + arrived[slot, c]

    def await_sent(k, left):
        s, c = k // chunks, k % chunks
        j = s if left else nw - 1 - s
        pltpu.make_async_copy(own(j, c), own(j, c), send_sem.at[j, c]).wait()

    def make_room(k, left=False):
        @pl.when(k >= chunks)
        def _():
            await_sent(k - window, left)

    pieces = (nw - 1) * chunks

    def line_step(k, carry):
        nearer = 2 * me < nw
        k_right = jnp.where(nearer, k, k - late)
        k_left = jnp.where(nearer, k - late, k)

        def forward(k, left):
            within = jnp.logical_and(k >= 0, k < pieces)
            s, c = jnp.maximum(k, 0) // chunks, jnp.maximum(k, 0) % chunks
            share_at = s if left else nw - 1 - s
            passes = me > share_at if left else me < share_at
            inner = me < nw - 1 if left else me > 0

            @pl.when(within & passes & (inner | (s > 0)))
            def _():
                @pl.when(inner)
                def _():
                    await_arrival(share_at, c)
                    add_arrived(share_at, share_at, c)

                make_room(k, left)
                (leftward if left else rightward)(share_at, c).start()

        forward(k_right, False)
        forward(k_left, True)
        return carry

    in_copies[0].wait()

    def chunk_step(c, carry):
        def place(r, carry):
            for q in range(per_chunk):
                value = tiles[slot_at[(c * per_chunk + q) * row_blocks + r]]
                value = jnp.log(jnp.maximum(value.astype(F32), 1.0)).astype(BF16)
                dense[pl.ds(pl.multiple_of(r * tile, tile), tile), q * tile : (q + 1) * tile] = value
            return carry

        lax.fori_loop(0, row_blocks, place, 0)

        @pl.when(c == 0)
        def _():
            in_copies[1].wait()

        def corange_rows(m, carry):
            at = pl.ds(pl.multiple_of(m * depth, depth), depth)
            part[c, at, :] = jnp.dot(psi[at, :], dense[...], preferred_element_type=F32)
            return carry

        lax.fori_loop(0, corank // depth, corange_rows, 0)

        @pl.when(me == 0)
        def _():
            rightward(nw - 1, c).start()

        @pl.when(me == nw - 1)
        def _():
            leftward(0, c).start()

        @pl.when(c >= lag)
        def _():
            line_step(c - lag, 0)

        @pl.when(c == 0)
        def _():
            in_copies[2].wait()

        chosen = omega[pl.ds(pl.multiple_of(c * width, width), width), :]

        def range_rows(m, carry):
            at = pl.ds(pl.multiple_of(m * tall, tall), tall)
            rpart[at, :] = rpart[at, :] + jnp.dot(dense[at, :], chosen, preferred_element_type=F32)
            return carry

        lax.fori_loop(0, rows // tall, range_rows, 0)
        return carry

    lax.fori_loop(0, chunks, chunk_step, 0)

    def range_copy(d):
        to = lax.rem(mine + d, nn)
        return pltpu.make_async_remote_copy(
            src_ref=rpart.at[pl.ds(pl.multiple_of(to * rblock, rblock), rblock)],
            dst_ref=rarrived.at[d - 1],
            send_sem=rsend_sem.at[d - 1], recv_sem=rrecv_sem.at[d - 1],
            device_id={"narrow": to}, device_id_type=MESH,
        )

    for d in range(1, nn):
        range_copy(d).start()

    lax.fori_loop(chunks - lag, pieces + late, line_step, 0)

    at = pl.ds(pl.multiple_of(mine * rblock, rblock), rblock)
    for d in range(1, nn):
        range_copy(d).wait_recv()
    total = rpart[at, :]
    for d in range(1, nn):
        total = total + rarrived[d - 1]
    rpart[at, :] = total
    range_out = pltpu.make_async_copy(rpart.at[at], range_hbm, rout_sem)
    range_out.start()

    def share_out(c):
        return pltpu.make_async_copy(
            own(me, c), corange_hbm.at[:, pl.ds(pl.multiple_of(c * width, width), width)], out_sem.at[c]
        )

    def finish(c, carry):
        @pl.when(me < nw - 1)
        def _():
            await_arrival(nw, c)
            add_arrived(me, nw, c)

        @pl.when(me > 0)
        def _():
            await_arrival(me, c)
            add_arrived(me, me, c)

        share_out(c).start()
        return carry

    lax.fori_loop(0, chunks, finish, 0)

    def drain(k, carry):
        for left, sent in ((False, (nw - 1 - me) * chunks), (True, me * chunks)):
            last = jnp.logical_and(k >= sent - window, k < sent)
            first = jnp.logical_and(k < chunks - window, k < sent)

            @pl.when(jnp.logical_or(first, last))
            def _():
                await_sent(k, left)

        return carry

    lax.fori_loop(0, (nw - 1) * chunks, drain, 0)

    def drain_out(c, carry):
        share_out(c).wait()
        return carry

    lax.fori_loop(0, chunks, drain_out, 0)
    for d in range(1, nn):
        range_copy(d).wait_send()
    range_out.wait()


def on_device(nw, nn, tiles, tile_rows, tile_cols, tile_live, omega, psi):
    slots, tile = tiles.shape[2], tiles.shape[3]
    rank, corank = omega.shape[1], psi.shape[0]
    rows, cols = psi.shape[1], omega.shape[0]
    row_blocks, col_blocks = rows // tile, cols // tile
    width = 4 * tile
    depth = 2 * tile
    tall = rows // 2
    window = 4
    lag = 1
    late = 2
    chunks = cols // width
    share, rblock = corank // nw, rows // nn

    place = jnp.where(tile_live > 0, tile_cols * row_blocks + tile_rows, -1).reshape(slots)
    hit = place[None, :] == jnp.arange(row_blocks * col_blocks, dtype=jnp.int32)[:, None]
    back = jnp.arange(slots, dtype=jnp.int32) - slots
    slot_at = slots + jnp.sum(jnp.where(hit, back[None, :], 0), axis=1, dtype=jnp.int32)

    return pl.pallas_call(
        functools.partial(kernel, nw, nn, width, depth, tall, window, lag, late),
        out_shape=(
            jax.ShapeDtypeStruct((rblock, rank), F32),
            pltpu.VMEM((share, cols), F32),
        ),
        in_specs=[pl.BlockSpec(memory_space=pltpu.SMEM)] + [pl.BlockSpec(memory_space=pl.ANY)] * 3,
        out_specs=(pl.BlockSpec(memory_space=pl.ANY), pl.BlockSpec(memory_space=pltpu.VMEM)),
        scratch_shapes=[
            pltpu.VMEM((slots + 1, tile, tile), BF16),
            pltpu.VMEM((corank, rows), BF16),
            pltpu.VMEM((cols, rank), BF16),
            pltpu.VMEM((rows, width), BF16),
            pltpu.VMEM((chunks, corank, width), F32),
            pltpu.VMEM((nw + 1, chunks, share, width), F32),
            pltpu.VMEM((rows, rank), F32),
            pltpu.VMEM((nn - 1, rblock, rank), F32),
            pltpu.SemaphoreType.DMA((3,)),
            pltpu.SemaphoreType.DMA((nw, chunks)),
            pltpu.SemaphoreType.DMA((nw + 1, chunks)),
            pltpu.SemaphoreType.DMA((nn - 1,)),
            pltpu.SemaphoreType.DMA((nn - 1,)),
            pltpu.SemaphoreType.DMA((chunks,)),
            pltpu.SemaphoreType.DMA,
        ],
        compiler_params=pltpu.CompilerParams(
            collective_id=0, has_side_effects=True, vmem_limit_bytes=52 << 20
        ),
        name="sketch",
    )(slot_at, tiles.reshape(slots, tile, tile), psi, omega)


def solution(mesh):
    in_specs = (
        P(("groups", "wide"), "narrow", None, None, None),
        P(("groups", "wide"), "narrow", None),
        P(("groups", "wide"), "narrow", None),
        P(("groups", "wide"), "narrow", None),
        P(("groups", "narrow"), None),
        P(None, ("groups", "wide")),
    )
    out_specs = (P(("groups", "wide", "narrow"), None), P("wide", ("groups", "narrow")))
    return jax.shard_map(
        functools.partial(on_device, mesh.shape["wide"], mesh.shape["narrow"]),
        mesh=mesh, in_specs=in_specs, out_specs=out_specs, check_vma=False,
    )
```
